256 devices in a mesh: rows: 16 (over z_hi, x), cols: 16 (over z_lo, y, core).
Axes of the slice: x: 4, y: 4, z: 8 (z_hi: 4, z_lo: 2; z = z_hi * 2 + z_lo), core: 2. Of those that a mesh axis runs over, the one named last changes fastest.
Arguments:
- frames: float32 [128, 16384], P(None, ('rows', 'cols')), may hold values from -6 to 6
- precision: float32 [16384, 16384], P('rows', 'cols'), as said below
Outputs:
- updated: float32 [16384, 16384], P('rows', 'cols')
- gradient: float32 [16384, 16384], P('rows', 'cols')
The draws below stay inside these ranges and needn't reach their ends.
Inputs may be any that keep to these rules, and one draw needn't show every extreme that they name: precision is symmetric; its diagonal lies between 1 and 4.
All inputs are finite; a program needn't handle non-finite values.
Results may differ from the reference program's by a relative error of at most 0.0001.
Values sent between devices are 32-bit elements; how exact they have to be, the bound alone decides.
No kernel may reach another device: no remote copies, remote signals or barrier semaphores. Data moves between devices by JAX's collectives and lax.ppermute only.
A program may use at most 128 MiB of HBM per device.

```python
import jax
import jax.numpy as jnp
from jax import lax

VARS = 16384
FRAMES = 128
ITERS = 3


def draw_precision(key, part):
    key = jax.random.fold_in(key, 11)
    first_key, second_key = jax.random.split(key)
    raw = jax.random.normal(first_key, (VARS, VARS), jnp.float32) * 0.05
    sym = (raw + raw.T) * 0.7071
    diag_vals = jax.random.uniform(second_key, (VARS,), jnp.float32, 1.0, 4.0)
    index = jnp.arange(VARS, dtype=jnp.int32)
    mask = index[:, None] == index[None, :]
    return jnp.where(mask, diag_vals[:, None], sym)


def block_scale(own_key, shape, cuts, smallest, top_value):
    gain = 1.0
    for position, parts in cuts:
        heights = jax.random.uniform(jax.random.fold_in(jax.random.fold_in(own_key, 6), position), (parts,), jnp.float32, smallest / len(cuts), top_value / len(cuts))
        gain = gain * jnp.repeat(jnp.exp(heights), shape[position] // parts).reshape((-1,) + (1,) * (len(shape) - 1 - position))
    return gain


def scatter_about(own_key, dims, deviation, limit, pieces=(), kind=jnp.bfloat16):
    factor_of = block_scale(own_key, dims, pieces, -0.22, 0.18) if pieces else 1.0
    values = jax.random.normal(own_key, dims, jnp.float32) * deviation * factor_of
    return jnp.minimum(jnp.maximum(values, -limit), limit).astype(kind)


def setup_inputs(seed: int = 0) -> dict:
    keys = jax.random.split(jax.random.key(seed), 3)
    return {
        "frames": scatter_about(keys[0], (FRAMES, VARS), 1.0, 6.0, ((1, 256),), jnp.float32),
        "precision": draw_precision(jax.random.fold_in(keys[2], 71), 0),
    }


step_size = 0.005
penalty = 4.0


def reference(frames, precision):
    highest = lax.Precision.HIGHEST
    index = jnp.arange(VARS, dtype=jnp.int32)
    mask = index[:, None] == index[None, :]
    current = precision
    gradient = jnp.zeros_like(precision)
    for sweep in range(ITERS):
        product = jnp.dot(current, frames.T, precision=highest, preferred_element_type=jnp.float32)
        weighted = jnp.dot(frames, current, precision=highest, preferred_element_type=jnp.float32)
        first = jnp.dot(product, frames, precision=highest, preferred_element_type=jnp.float32)
        second = jnp.dot(frames.T, weighted, precision=highest, preferred_element_type=jnp.float32)
        inverse = jnp.where(mask, 1.0 / jnp.where(mask, current, 1.0), 0.0)
        gradient = (first + second) * (0.5 / FRAMES) - inverse
        moved = current - step_size * gradient
        bound = step_size * penalty
        current = jnp.where(mask, moved, moved - jnp.clip(moved, -bound, bound))
    return current, gradient
```

```python
import functools

import jax
import jax.numpy as jnp
from jax import lax
from jax.experimental import pallas as pl
from jax.experimental.pallas import tpu as pltpu
from jax.sharding import PartitionSpec as P

ITERS = 3

step_size = 0.005
penalty = 4.0

SIDE = 16
PIECE = 64
TILE = 256
NT = (((1,), (1,)), ((), ()))


def split(value):
    high = value.astype(jnp.bfloat16)
    low = (value - high.astype(jnp.float32)).astype(jnp.bfloat16)
    return high, low


def dot(a, b, dims=(((1,), (0,)), ((), ()))):
    return lax.dot_general(a, b, dims, preferred_element_type=jnp.float32)


def kernel(update, emit_sums, emit_grad, frame_count, *refs):
    refs = list(refs)
    place = refs.pop(0)
    omega = refs.pop(0)
    xc = refs.pop(0)
    if update:
        xr, yr, yc = refs.pop(0), refs.pop(0), refs.pop(0)
        out = refs.pop(0)
    grad = refs.pop(0) if emit_grad else None
    sums = refs.pop(0) if emit_sums else None
    if update:
        ah, al, bh, bl = refs.pop(0), refs.pop(0), refs.pop(0), refs.pop(0)
    xx = refs.pop(0) if emit_sums else None
    if update and not emit_grad:
        grad = refs.pop(0)
    rows = omega.shape[1]
    tile = pl.program_id(0)
    row, col = place[0], place[1]

    @pl.when(tile == 0)
    def _():
        for q in range(SIDE):
            span = pl.ds(q * PIECE, PIECE)
            high, low = split(xc[q])
            if emit_sums:
                xx[span, :frame_count] = high
                xx[span, frame_count:] = low
            if update:
                bh[span, :frame_count] = high
                bl[span, :frame_count] = low
                high, low = split(yc[q])
                bh[span, frame_count:] = high
                bl[span, frame_count:] = low
                d = q ^ col
                slot = (d & 1) * 8 + ((d >> 1) & 3) * 2 + (d >> 3)
                high, low = split(yr[slot])
                ah[span, :frame_count] = high
                al[span, :frame_count] = low
                high, low = split(xr[slot])
                ah[span, frame_count:] = high
                al[span, frame_count:] = low

    chunks = [slice(j, j + TILE) for j in range(0, rows, TILE)]
    bound = step_size * penalty
    if update:
        mine = pl.ds(tile * TILE, TILE)
        a_high, a_low = ah[mine, :], al[mine, :]
        for j in chunks:
            total = dot(a_high, bh[j, :], NT) + dot(a_high, bl[j, :], NT) + dot(a_low, bh[j, :], NT)
            g = total * (0.5 / frame_count)
            grad[:, j] = g
            moved = omega[:, j] - step_size * g
            out[:, j] = moved - jnp.clip(moved, -bound, bound)

        @pl.when(row == col)
        def _():
            here = pl.ds(tile * TILE, TILE)
            eye = lax.broadcasted_iota(jnp.int32, (TILE, TILE), 0) == lax.broadcasted_iota(jnp.int32, (TILE, TILE), 1)
            old = omega[:, here]
            g = grad[:, here] - jnp.where(eye, 1.0 / jnp.where(eye, old, 1.0), 0.0)
            grad[:, here] = g
            moved = old - step_size * g
            out[:, here] = jnp.where(eye, moved, moved - jnp.clip(moved, -bound, bound))

    if emit_sums:
        source = out if update else omega
        both = jnp.zeros((TILE, 2 * frame_count), jnp.float32)
        rest = jnp.zeros((TILE, frame_count), jnp.float32)
        for j in chunks:
            high, low = split(source[:, j])
            both += dot(high, xx[j, :])
            rest += dot(low, xx[j, :frame_count])
        total = both[:, :frame_count] + both[:, frame_count:] + rest
        for s in range(TILE // PIECE):
            q = tile * (TILE // PIECE) + s
            slot = ((q ^ col) & 1) * 8 + (q >> 3) * 4 + ((q >> 1) & 3)
            sums[slot] = total[s * PIECE : (s + 1) * PIECE]


def sweep(place, omega, xc, panels, emit_sums, emit_grad):
    update = bool(panels)
    rows = omega.shape[0]
    frame_count = xc.shape[-1]
    block = pl.BlockSpec((TILE, rows), lambda i, *_: (i, 0))
    whole = pl.BlockSpec((SIDE, PIECE, frame_count), lambda i, *_: (0, 0, 0))
    matrix = jax.ShapeDtypeStruct(omega.shape, jnp.float32)
    shapes, specs, scratch = [], [], []
    if update:
        shapes.append(matrix)
        specs.append(block)
        scratch += [pltpu.VMEM((rows, 2 * frame_count), jnp.bfloat16)] * 4
    if emit_grad:
        shapes.append(matrix)
        specs.append(block)
    if emit_sums:
        shapes.append(jax.ShapeDtypeStruct((SIDE, PIECE, frame_count), jnp.float32))
        specs.append(whole)
        scratch.append(pltpu.VMEM((rows, 2 * frame_count), jnp.bfloat16))
    if update and not emit_grad:
        scratch.append(pltpu.VMEM((TILE, rows), jnp.float32))
    return pl.pallas_call(
        functools.partial(kernel, update, emit_sums, emit_grad, frame_count),
        out_shape=shapes,
        grid_spec=pltpu.PrefetchScalarGridSpec(
            num_scalar_prefetch=1,
            grid=(rows // TILE,),
            in_specs=[block, whole] + [whole] * len(panels),
            out_specs=specs,
            scratch_shapes=scratch,
        ),
        compiler_params=pltpu.CompilerParams(vmem_limit_bytes=28 * 1024 * 1024),
        cost_estimate=pl.CostEstimate(flops=4 * rows * rows * frame_count * 3, bytes_accessed=8 * rows * rows, transcendentals=0),
    )(place, omega, xc, *panels)


def swap_cols(value, mask):
    return lax.ppermute(value, "cols", [(i, i ^ mask) for i in range(SIDE)])


EIGHTS = [[k + 2 * y + 8 * z for z in range(2) for y in range(4)] for k in range(2)]


def scatter_sum(sums):
    near = sums[:8] + swap_cols(sums[8:], 1)
    return lax.all_to_all(near, "cols", 0, 0, axis_index_groups=EIGHTS).sum(0)


def gather_cols(piece):
    value = piece[None]
    value = jnp.concatenate([value, swap_cols(value, 8)], 0)
    value = jnp.concatenate([value] + [swap_cols(value, 2 * m) for m in (1, 2, 3)], 0)
    return jnp.concatenate([value, swap_cols(value, 1)], 0)


def gather_turned(piece):
    turn = [(r * SIDE + c, c * SIDE + r) for r in range(SIDE) for c in range(SIDE)]
    turned = lax.ppermute(piece, ("rows", "cols"), turn)
    return lax.all_to_all(jnp.broadcast_to(turned, (SIDE,) + piece.shape), "rows", 0, 0)


def on_device(frames, precision):
    place = jnp.stack([lax.axis_index("rows"), lax.axis_index("cols")]).astype(jnp.int32)
    own = frames.T
    xc = gather_turned(own)
    xr = gather_cols(own)
    (sums,) = sweep(place, precision, xc, (), True, False)
    current = precision
    for index in range(ITERS):
        piece = scatter_sum(sums)
        yc = gather_turned(piece)
        yr = gather_cols(piece)
        if index < ITERS - 1:
            current, sums = sweep(place, current, xc, (xr, yr, yc), True, False)
        else:
            current, gradient = sweep(place, current, xc, (xr, yr, yc), False, True)
    return (current, gradient)


def solution(mesh):
    placed = (P(None, ("rows", "cols")), P("rows", "cols"))
    return jax.shard_map(
        on_device,
        mesh=mesh,
        in_specs=placed,
        out_specs=(P("rows", "cols"), P("rows", "cols")),
        check_vma=False,
    )
```

```python
import functools

import jax
import jax.numpy as jnp
import numpy as np
from jax import lax
from jax.experimental import pallas as pl
from jax.experimental.pallas import tpu as pltpu
from jax.sharding import PartitionSpec as P

ITERS = 3

step_size = 0.005
penalty = 4.0

SIDE = 16
PIECE = 64
TILE = 256
NT = (((1,), (1,)), ((), ()))


def split(value):
    high = value.astype(jnp.bfloat16)
    low = (value - high.astype(jnp.float32)).astype(jnp.bfloat16)
    return high, low


def dot(a, b, dims=(((1,), (0,)), ((), ()))):
    return lax.dot_general(a, b, dims, preferred_element_type=jnp.float32)


def kernel(update, emit_sums, emit_grad, frame_count, *refs):
    refs = list(refs)
    place = refs.pop(0)
    omega = refs.pop(0)
    xc = refs.pop(0)
    if update:
        xr, yr, yc = refs.pop(0), refs.pop(0), refs.pop(0)
        out = refs.pop(0)
    grad = refs.pop(0) if emit_grad else None
    sums = refs.pop(0) if emit_sums else None
    if update:
        ah, al, bh, bl = refs.pop(0), refs.pop(0), refs.pop(0), refs.pop(0)
    xx = refs.pop(0) if emit_sums else None
    if update and not emit_grad:
        grad = refs.pop(0)
    rows = omega.shape[1]
    tile = pl.program_id(0)
    row, col = place[0], place[1]

    @pl.when(tile == 0)
    def _():
        for q in range(SIDE):
            span = pl.ds(q * PIECE, PIECE)
            high, low = split(xc[place[2 + q]])
            if emit_sums:
                xx[span, :frame_count] = high
                xx[span, frame_count:] = low
            if update:
                bh[span, :frame_count] = high
                bl[span, :frame_count] = low
                high, low = split(yc[place[34 + q]])
                bh[span, frame_count:] = high
                bl[span, frame_count:] = low
                high, low = split(yr[place[50 + q]])
                ah[span, :frame_count] = high
                al[span, :frame_count] = low
                high, low = split(xr[place[18 + q]])
                ah[span, frame_count:] = high
                al[span, frame_count:] = low

    chunks = [slice(j, j + TILE) for j in range(0, rows, TILE)]
    bound = step_size * penalty
    if update:
        mine = pl.ds(tile * TILE, TILE)
        a_high, a_low = ah[mine, :], al[mine, :]
        for j in chunks:
            total = dot(a_high, bh[j, :], NT) + dot(a_high, bl[j, :], NT) + dot(a_low, bh[j, :], NT)
            g = total * (0.5 / frame_count)
            grad[:, j] = g
            moved = omega[:, j] - step_size * g
            out[:, j] = moved - jnp.clip(moved, -bound, bound)

        @pl.when(row == col)
        def _():
            here = pl.ds(tile * TILE, TILE)
            eye = lax.broadcasted_iota(jnp.int32, (TILE, TILE), 0) == lax.broadcasted_iota(jnp.int32, (TILE, TILE), 1)
            old = omega[:, here]
            g = grad[:, here] - jnp.where(eye, 1.0 / jnp.where(eye, old, 1.0), 0.0)
            grad[:, here] = g
            moved = old - step_size * g
            out[:, here] = jnp.where(eye, moved, moved - jnp.clip(moved, -bound, bound))

    if emit_sums:
        source = out if update else omega
        both = jnp.zeros((TILE, 2 * frame_count), jnp.float32)
        rest = jnp.zeros((TILE, frame_count), jnp.float32)
        for j in chunks:
            high, low = split(source[:, j])
            both += dot(high, xx[j, :])
            rest += dot(low, xx[j, :frame_count])
        total = both[:, :frame_count] + both[:, frame_count:] + rest
        for s in range(TILE // PIECE):
            q = tile * (TILE // PIECE) + s
            slot = ((q ^ col) & 1) * 8 + ((q ^ col) >> 3) * 4 + ((q >> 1) & 3)
            sums[slot] = total[s * PIECE : (s + 1) * PIECE]


def sweep(place, omega, xc, panels, emit_sums, emit_grad):
    update = bool(panels)
    rows = omega.shape[0]
    frame_count = xc.shape[-1]
    block = pl.BlockSpec((TILE, rows), lambda i, *_: (i, 0))
    whole = pl.BlockSpec((SIDE, PIECE, frame_count), lambda i, *_: (0, 0, 0))
    matrix = pltpu.HBM(omega.shape, jnp.float32)
    shapes, specs, scratch = [], [], []
    if update:
        shapes.append(matrix)
        specs.append(block)
        scratch += [pltpu.VMEM((rows, 2 * frame_count), jnp.bfloat16)] * 4
    if emit_grad:
        shapes.append(matrix)
        specs.append(block)
    if emit_sums:
        shapes.append(jax.ShapeDtypeStruct((SIDE, PIECE, frame_count), jnp.float32))
        specs.append(whole)
        scratch.append(pltpu.VMEM((rows, 2 * frame_count), jnp.bfloat16))
    if update and not emit_grad:
        scratch.append(pltpu.VMEM((TILE, rows), jnp.float32))
    return pl.pallas_call(
        functools.partial(kernel, update, emit_sums, emit_grad, frame_count),
        out_shape=shapes,
        grid_spec=pltpu.PrefetchScalarGridSpec(
            num_scalar_prefetch=1,
            grid=(rows // TILE,),
            in_specs=[block, whole] + [whole] * len(panels),
            out_specs=specs,
            scratch_shapes=scratch,
        ),
        compiler_params=pltpu.CompilerParams(vmem_limit_bytes=28 * 1024 * 1024),
        cost_estimate=pl.CostEstimate(flops=4 * rows * rows * frame_count * 3, bytes_accessed=8 * rows * rows, transcendentals=0),
    )(place, pltpu.with_memory_space_constraint(omega, pltpu.HBM), xc, *panels)


def swap_cols(value, mask):
    return lax.ppermute(value, "cols", [(i, i ^ mask) for i in range(SIDE)])


def swap_rows(value, mask):
    return lax.ppermute(value, "rows", [(i, i ^ mask) for i in range(SIDE)])


def landing(r, c):
    high, x = r >> 2, r & 3
    low, y, core = c >> 3, (c >> 1) & 3, c & 1
    off = (2, 1, 0, 3)[(y - ((r >> 1) & 3)) % 4]
    far = [min(d % 8, -d % 8) for d in (2 * off + (r >> 3), 2 * off + (r >> 3) - 1)]
    if far[low] > far[1 - low] or (far[0] == far[1] and low == 0):
        step = (0, 1)[core]
    else:
        step = (3, 2)[core]
    return ((high + off) % 4) * 4 + (x + step) % 4, r


LANDING = {(r, c): landing(r, c) for r in range(SIDE) for c in range(SIDE)}
SOURCE = {there: here for here, there in LANDING.items()}


def slots():
    table = np.zeros((SIDE, SIDE, 4, SIDE), np.int32)
    for r in range(SIDE):
        for c in range(SIDE):
            for q in range(SIDE):
                lands = LANDING[c, (q & 9) | (SOURCE[r, c][1] & 6)][0]
                hop = (lands ^ r) & 3
                y, mine = (q >> 1) & 3, (SOURCE[r, c][1] >> 1) & 3
                side = ((q ^ c) & 1) * 8 + ((q ^ c) >> 3) * 4
                table[r, c, 0, q] = hop * 4 + (y ^ mine)
                table[r, c, 1, q] = side + (y ^ ((c >> 1) & 3))
                table[r, c, 2, q] = hop * 4 + y
                table[r, c, 3, q] = side + y
    return table.reshape(SIDE, SIDE, 4 * SIDE)


def sum_near(sums):
    value = sums[:8] + swap_cols(sums[8:], 1)
    value = value[:4] + swap_cols(value[4:], 8)
    others = [swap_cols(value, 2 * m) for m in (1, 2, 3)]
    return (value + others[0]) + (others[1] + others[2])


def gather_near(piece):
    value = piece[None]
    return jnp.concatenate([value] + [swap_cols(value, 2 * m) for m in (1, 2, 3)], 0)


def panels_of(four):
    pairs = [(r * SIDE + c, LANDING[r, c][0] * SIDE + LANDING[r, c][1]) for r in range(SIDE) for c in range(SIDE)]
    turned = lax.ppermute(four, ("rows", "cols"), pairs)
    across = jnp.concatenate([turned] + [swap_rows(turned, m) for m in (1, 2, 3)], 0)
    along = jnp.concatenate([four, swap_cols(four, 8)], 0)
    along = jnp.concatenate([along, swap_cols(along, 1)], 0)
    return across, along


def on_device(frames, precision):
    row, col = lax.axis_index("rows"), lax.axis_index("cols")
    table = lax.dynamic_slice(jnp.asarray(slots()), (row, col, 0), (1, 1, 4 * SIDE)).reshape(-1)
    place = jnp.concatenate([jnp.stack([row, col]).astype(jnp.int32), table])
    xc, xr = panels_of(gather_near(frames.T))
    (sums,) = sweep(place, precision, xc, (), True, False)
    current = precision
    for index in range(ITERS):
        yc, yr = panels_of(sum_near(sums))
        if index < ITERS - 1:
            current, sums = sweep(place, current, xc, (xr, yr, yc), True, False)
        else:
            current, gradient = sweep(place, current, xc, (xr, yr, yc), False, True)
    return (current, gradient)


def solution(mesh):
    placed = (P(None, ("rows", "cols")), P("rows", "cols"))
    return jax.shard_map(
        on_device,
        mesh=mesh,
        in_specs=placed,
        out_specs=(P("rows", "cols"), P("rows", "cols")),
        check_vma=False,
    )
```

```python
import functools

import jax
import jax.numpy as jnp
import numpy as np
from jax import lax
from jax.experimental import pallas as pl
from jax.experimental.pallas import tpu as pltpu
from jax.sharding import PartitionSpec as P

ITERS = 3

step_size = 0.005
penalty = 4.0

SIDE = 16
PIECE = 64
TILE = 512
FETCHES = 8
NT = (((1,), (1,)), ((), ()))


def split(value):
    high = value.astype(jnp.bfloat16)
    low = (value - high.astype(jnp.float32)).astype(jnp.bfloat16)
    return high, low


def dot(a, b, dims=(((1,), (0,)), ((), ()))):
    return lax.dot_general(a, b, dims, preferred_element_type=jnp.float32)


def load_panels(update, emit_sums, frame_count, place, xc, xr, yr, yc, ah, al, bh, bl, xx):
    for q in range(SIDE):
        span = pl.ds(q * PIECE, PIECE)
        high, low = split(xc[place[2 + q]])
        if emit_sums:
            xx[span, :frame_count] = high
            xx[span, frame_count:] = low
        if update:
            bh[span, :frame_count] = high
            bl[span, :frame_count] = low
            high, low = split(yc[place[34 + q]])
            bh[span, frame_count:] = high
            bl[span, frame_count:] = low
            high, low = split(yr[place[50 + q]])
            ah[span, :frame_count] = high
            al[span, :frame_count] = low
            high, low = split(xr[place[18 + q]])
            ah[span, frame_count:] = high
            al[span, frame_count:] = low


def gradient_part(frame_count, a_high, a_low, b_high, b_low):
    return (dot(a_high, b_high, NT) + dot(a_high, b_low, NT) + dot(a_low, b_high, NT)) * (0.5 / frame_count)


def step(old, g, eye):
    bound = step_size * penalty
    if eye is not None:
        g = g - jnp.where(eye, 1.0 / jnp.where(eye, old, 1.0), 0.0)
    moved = old - step_size * g
    cut = jnp.clip(moved, -bound, bound)
    if eye is not None:
        cut = jnp.where(eye, 0.0, cut)
    return g, moved - cut


def diagonal(on):
    eye = lax.broadcasted_iota(jnp.int32, (TILE, TILE), 0) == lax.broadcasted_iota(jnp.int32, (TILE, TILE), 1)
    return jnp.logical_and(eye, on)


def sweep_kernel(update, frame_count, *refs):
    if update:
        place, omega, xc, xr, yr, yc, out, sums, ah, al, bh, bl, xx = refs
        load_panels(True, True, frame_count, place, xc, xr, yr, yc, ah, al, bh, bl, xx)
    else:
        place, whole, xc, omega, sums, xx, arrived = refs
        step_rows = whole.shape[0] // FETCHES
        fetches = []
        for n in range(FETCHES):
            part = pl.ds(n * step_rows, step_rows)
            fetches.append(pltpu.make_async_copy(whole.at[part, :], omega.at[part, :], arrived.at[n]))
            fetches[-1].start()
        load_panels(False, True, frame_count, place, xc, None, None, None, None, None, None, None, xx)
    rows = omega.shape[0]
    col = place[1]
    here = place[0] == col
    for t in range(rows // TILE):
        mine = slice(t * TILE, t * TILE + TILE)
        both = rest = None
        if not update:
            for n in range(t * TILE // step_rows, (t + 1) * TILE // step_rows):
                fetches[n].wait()
        for j in range(rows // TILE):
            span = slice(j * TILE, j * TILE + TILE)
            value = omega[mine, span]
            if update:
                g = gradient_part(frame_count, ah[mine, :], al[mine, :], bh[span, :], bl[span, :])
                _, value = step(value, g, diagonal(here) if j == t else None)
                out[mine, span] = value
            high, low = split(value)
            first = dot(high, xx[span, :])
            second = dot(low, xx[span, :frame_count])
            both = first if both is None else both + first
            rest = second if rest is None else rest + second
        total = both[:, :frame_count] + both[:, frame_count:] + rest
        for s in range(TILE // PIECE):
            q = t * (TILE // PIECE) + s
            slot = ((q ^ col) & 1) * 8 + ((q ^ col) >> 3) * 4 + ((q >> 1) & 3)
            sums[slot] = total[s * PIECE : (s + 1) * PIECE]


def sweep(place, omega, xc, panels):
    update = bool(panels)
    rows = omega.shape[0]
    frame_count = xc.shape[-1]
    wide = pltpu.VMEM((rows, 2 * frame_count), jnp.bfloat16)
    vmem = pl.BlockSpec(memory_space=pltpu.VMEM)
    shapes = [pltpu.VMEM(omega.shape, jnp.float32), jax.ShapeDtypeStruct((SIDE, PIECE, frame_count), jnp.float32)]
    home = pltpu.VMEM if update else pltpu.HBM
    return pl.pallas_call(
        functools.partial(sweep_kernel, update, frame_count),
        out_shape=shapes,
        in_specs=[pl.BlockSpec(memory_space=pltpu.SMEM), pl.BlockSpec(memory_space=home)] + [vmem] * (1 + len(panels)),
        out_specs=[vmem] * 2,
        scratch_shapes=[wide] * 5 if update else [wide, pltpu.SemaphoreType.DMA((FETCHES,))],
        compiler_params=pltpu.CompilerParams(vmem_limit_bytes=28 * 1024 * 1024),
        cost_estimate=pl.CostEstimate(flops=4 * rows * rows * frame_count * 3, bytes_accessed=8 * rows * rows, transcendentals=0),
    )(place, pltpu.with_memory_space_constraint(omega, home), xc, *panels)


def final_kernel(frame_count, place, omega, xc, xr, yr, yc, out, grad, ah, al, bh, bl, values, grads, sent):
    load_panels(True, False, frame_count, place, xc, xr, yr, yc, ah, al, bh, bl, None)
    rows = omega.shape[0]
    here = place[0] == place[1]
    copies = []
    for t in range(rows // TILE):
        mine = slice(t * TILE, t * TILE + TILE)
        for j in range(rows // TILE):
            span = slice(j * TILE, j * TILE + TILE)
            g = gradient_part(frame_count, ah[mine, :], al[mine, :], bh[span, :], bl[span, :])
            g, value = step(omega[mine, span], g, diagonal(here) if j == t else None)
            grads[mine, span] = g
            values[mine, span] = value
            for held, there in ((grads, grad), (values, out)):
                block = (pl.ds(t * TILE, TILE), pl.ds(j * TILE, TILE))
                copies.append(pltpu.make_async_copy(held.at[block], there.at[block], sent.at[len(copies)]))
                copies[-1].start()
    for copy in copies:
        copy.wait()


def final_sweep(place, omega, xc, panels):
    rows = omega.shape[0]
    frame_count = xc.shape[-1]
    wide = pltpu.VMEM((rows, 2 * frame_count), jnp.bfloat16)
    vmem = pl.BlockSpec(memory_space=pltpu.VMEM)
    return pl.pallas_call(
        functools.partial(final_kernel, frame_count),
        out_shape=[pltpu.HBM(omega.shape, jnp.float32)] * 2,
        in_specs=[pl.BlockSpec(memory_space=pltpu.SMEM)] + [vmem] * (2 + len(panels)),
        out_specs=[pl.BlockSpec(memory_space=pltpu.HBM)] * 2,
        scratch_shapes=[wide] * 4
        + [pltpu.VMEM(omega.shape, jnp.float32)] * 2
        + [pltpu.SemaphoreType.DMA((2 * (rows // TILE) ** 2,))],
        compiler_params=pltpu.CompilerParams(vmem_limit_bytes=28 * 1024 * 1024),
        cost_estimate=pl.CostEstimate(flops=4 * rows * rows * frame_count * 3, bytes_accessed=12 * rows * rows, transcendentals=0),
    )(place, pltpu.with_memory_space_constraint(omega, pltpu.VMEM), xc, *panels)


def swap_cols(value, mask):
    return lax.ppermute(value, "cols", [(i, i ^ mask) for i in range(SIDE)])


def swap_rows(value, mask):
    return lax.ppermute(value, "rows", [(i, i ^ mask) for i in range(SIDE)])


ROWS = (
    "b9f71c52ea83046d",
    "a864d20fcb1e5397",
    "5ca9e4128bf07d36",
    "6fd8b3071a9ce542",
    "70259fcb68ade134",
    "4187ea2d950cf36b",
    "e075398f42abd61c",
    "b1264acd5f8739e0",
    "d23f58b4610a9ce7",
    "7ea018d6235fcb94",
    "a4c0296ed7135fb8",
    "35d18f7bac2460e9",
    "9fe4601bcd2875a3",
    "ca5d3782efb14609",
    "17e8ad43f92c60b5",
    "60fb9c25e83d71a4",
)


LANDING = {(r, c): (int(ROWS[r][c], SIDE), r) for r in range(SIDE) for c in range(SIDE)}
SOURCE = {there: here for here, there in LANDING.items()}


def slots():
    table = np.zeros((SIDE, SIDE, 4, SIDE), np.int32)
    for r in range(SIDE):
        for c in range(SIDE):
            found = {}
            for hop in range(4):
                near = SOURCE[r ^ hop, c][1]
                for y in range(4):
                    found[near & 9 | y << 1] = hop * 4 + y, hop * 4 + (y ^ (near >> 1 & 3))
            for q in range(SIDE):
                y = (q >> 1) & 3
                side = ((q ^ c) & 1) * 8 + ((q ^ c) >> 3) * 4
                table[r, c, 0, q] = found[q][1]
                table[r, c, 1, q] = side + (y ^ ((c >> 1) & 3))
                table[r, c, 2, q] = found[q][0]
                table[r, c, 3, q] = side + y
    return table.reshape(SIDE, SIDE, 4 * SIDE)


def sum_near(sums):
    value = sums[:8] + swap_cols(sums[8:], 1)
    value = value[:4] + swap_cols(value[4:], 8)
    others = [swap_cols(value, 2 * m) for m in (1, 2, 3)]
    return (value + others[0]) + (others[1] + others[2])


def gather_near(piece):
    value = piece[None]
    return jnp.concatenate([value] + [swap_cols(value, 2 * m) for m in (1, 2, 3)], 0)


def turn(four):
    pairs = [(r * SIDE + c, LANDING[r, c][0] * SIDE + LANDING[r, c][1]) for r in range(SIDE) for c in range(SIDE)]
    turned = lax.ppermute(four, ("rows", "cols"), pairs)
    return jnp.concatenate([turned] + [swap_rows(turned, m) for m in (1, 2, 3)], 0)


def along(four):
    value = jnp.concatenate([four, swap_cols(four, 8)], 0)
    return jnp.concatenate([value, swap_cols(value, 1)], 0)


def on_device(frames, precision):
    row, col = lax.axis_index("rows"), lax.axis_index("cols")
    table = lax.dynamic_slice(jnp.asarray(slots()), (row, col, 0), (1, 1, 4 * SIDE)).reshape(-1)
    place = jnp.concatenate([jnp.stack([row, col]).astype(jnp.int32), table])
    own = gather_near(frames.T)
    xc = turn(own)
    xr = along(own)
    current, sums = sweep(place, precision, xc, ())
    for index in range(ITERS):
        four = sum_near(sums)
        yc = turn(four)
        yr = along(four)
        if index < ITERS - 1:
            current, sums = sweep(place, current, xc, (xr, yr, yc))
        else:
            current, gradient = final_sweep(place, current, xc, (xr, yr, yc))
    return (current, gradient)


def solution(mesh):
    placed = (P(None, ("rows", "cols")), P("rows", "cols"))
    return jax.shard_map(
        on_device,
        mesh=mesh,
        in_specs=placed,
        out_specs=(P("rows", "cols"), P("rows", "cols")),
        check_vma=False,
    )
```

```python
import functools

import jax
import jax.numpy as jnp
import numpy as np
from jax import lax
from jax.experimental import pallas as pl
from jax.experimental.pallas import tpu as pltpu
from jax.sharding import PartitionSpec as P

ITERS = 3

step_size = 0.005
penalty = 4.0

SIDE = 16
PIECE = 64
TILE = 512
FETCHES = 8
NT = (((1,), (1,)), ((), ()))


def split(value):
    high = value.astype(jnp.bfloat16)
    low = (value - high.astype(jnp.float32)).astype(jnp.bfloat16)
    return high, low


def dot(a, b, dims=(((1,), (0,)), ((), ()))):
    return lax.dot_general(a, b, dims, preferred_element_type=jnp.float32)


def load_panels(update, emit_sums, frame_count, place, xc, xr, yr, yc, ah, al, bh, bl, xx):
    for q in range(SIDE):
        span = pl.ds(q * PIECE, PIECE)
        high, low = split(xc[place[2 + q]])
        if emit_sums:
            xx[span, :frame_count] = high
            xx[span, frame_count:] = low
        if update:
            bh[span, :frame_count] = high
            bl[span, :frame_count] = low
            high, low = split(yc[place[34 + q]])
            bh[span, frame_count:] = high
            bl[span, frame_count:] = low
            high, low = split(yr[place[50 + q]])
            ah[span, :frame_count] = high
            al[span, :frame_count] = low
            high, low = split(xr[place[18 + q]])
            ah[span, frame_count:] = high
            al[span, frame_count:] = low


def gradient_part(frame_count, a_high, a_low, b_high, b_low):
    return (dot(a_high, b_high, NT) + dot(a_high, b_low, NT) + dot(a_low, b_high, NT)) * (0.5 / frame_count)


def step(old, g, eye):
    bound = step_size * penalty
    if eye is not None:
        g = g - jnp.where(eye, 1.0 / jnp.where(eye, old, 1.0), 0.0)
    moved = old - step_size * g
    cut = jnp.clip(moved, -bound, bound)
    if eye is not None:
        cut = jnp.where(eye, 0.0, cut)
    return g, moved - cut


def diagonal(on):
    eye = lax.broadcasted_iota(jnp.int32, (TILE, TILE), 0) == lax.broadcasted_iota(jnp.int32, (TILE, TILE), 1)
    return jnp.logical_and(eye, on)


def sweep_kernel(update, frame_count, *refs):
    if update:
        place, omega, xc, xr, yr, yc, out, sums, ah, al, bh, bl, xx = refs
        load_panels(True, True, frame_count, place, xc, xr, yr, yc, ah, al, bh, bl, xx)
    else:
        place, omega, xc, sums, xx = refs
        load_panels(False, True, frame_count, place, xc, None, None, None, None, None, None, None, xx)
    rows = omega.shape[0]
    col = place[1]
    here = place[0] == col
    for t in range(rows // TILE):
        mine = slice(t * TILE, t * TILE + TILE)
        both = rest = None
        for j in range(rows // TILE):
            span = slice(j * TILE, j * TILE + TILE)
            value = omega[mine, span]
            if update:
                g = gradient_part(frame_count, ah[mine, :], al[mine, :], bh[span, :], bl[span, :])
                _, value = step(value, g, diagonal(here) if j == t else None)
                out[mine, span] = value
            high, low = split(value)
            first = dot(high, xx[span, :])
            second = dot(low, xx[span, :frame_count])
            both = first if both is None else both + first
            rest = second if rest is None else rest + second
        total = both[:, :frame_count] + both[:, frame_count:] + rest
        for s in range(TILE // PIECE):
            q = t * (TILE // PIECE) + s
            slot = ((q ^ col) & 1) * 8 + ((q ^ col) >> 3) * 4 + ((q >> 1) & 3)
            sums[slot] = total[s * PIECE : (s + 1) * PIECE]


def sweep(place, omega, xc, panels):
    update = bool(panels)
    rows = omega.shape[0]
    frame_count = xc.shape[-1]
    wide = pltpu.VMEM((rows, 2 * frame_count), jnp.bfloat16)
    vmem = pl.BlockSpec(memory_space=pltpu.VMEM)
    shapes = [jax.ShapeDtypeStruct((SIDE, PIECE, frame_count), jnp.float32)]
    if update:
        shapes = [pltpu.VMEM(omega.shape, jnp.float32)] + shapes
    return pl.pallas_call(
        functools.partial(sweep_kernel, update, frame_count),
        out_shape=shapes,
        in_specs=[pl.BlockSpec(memory_space=pltpu.SMEM)] + [vmem] * (2 + len(panels)),
        out_specs=[vmem] * len(shapes),
        scratch_shapes=[wide] * (5 if update else 1),
        compiler_params=pltpu.CompilerParams(vmem_limit_bytes=28 * 1024 * 1024),
        cost_estimate=pl.CostEstimate(flops=4 * rows * rows * frame_count * 3, bytes_accessed=8 * rows * rows, transcendentals=0),
    )(place, pltpu.with_memory_space_constraint(omega, pltpu.VMEM), xc, *panels)


def stage_kernel(whole, held, arrived):
    step_rows = whole.shape[0] // FETCHES
    copies = []
    for n in range(FETCHES):
        part = pl.ds(n * step_rows, step_rows)
        copies.append(pltpu.make_async_copy(whole.at[part, :], held.at[part, :], arrived.at[n]))
        copies[-1].start()
    for copy in copies:
        copy.wait()


def staged(omega):
    return pl.pallas_call(
        stage_kernel,
        out_shape=pltpu.VMEM(omega.shape, jnp.float32),
        in_specs=[pl.BlockSpec(memory_space=pltpu.HBM)],
        out_specs=pl.BlockSpec(memory_space=pltpu.VMEM),
        scratch_shapes=[pltpu.SemaphoreType.DMA((FETCHES,))],
        compiler_params=pltpu.CompilerParams(vmem_limit_bytes=4 * 1024 * 1024),
        cost_estimate=pl.CostEstimate(flops=0, bytes_accessed=8 * omega.size, transcendentals=0),
    )(pltpu.with_memory_space_constraint(omega, pltpu.HBM))


def final_kernel(frame_count, place, omega, xc, xr, yr, yc, out, grad, ah, al, bh, bl, values, grads, sent):
    load_panels(True, False, frame_count, place, xc, xr, yr, yc, ah, al, bh, bl, None)
    rows = omega.shape[0]
    here = place[0] == place[1]
    copies = []
    for t in range(rows // TILE):
        mine = slice(t * TILE, t * TILE + TILE)
        for j in range(rows // TILE):
            span = slice(j * TILE, j * TILE + TILE)
            g = gradient_part(frame_count, ah[mine, :], al[mine, :], bh[span, :], bl[span, :])
            g, value = step(omega[mine, span], g, diagonal(here) if j == t else None)
            grads[mine, span] = g
            values[mine, span] = value
            for held, there in ((grads, grad), (values, out)):
                block = (pl.ds(t * TILE, TILE), pl.ds(j * TILE, TILE))
                copies.append(pltpu.make_async_copy(held.at[block], there.at[block], sent.at[len(copies)]))
                copies[-1].start()
    for copy in copies:
        copy.wait()


def final_sweep(place, omega, xc, panels):
    rows = omega.shape[0]
    frame_count = xc.shape[-1]
    wide = pltpu.VMEM((rows, 2 * frame_count), jnp.bfloat16)
    vmem = pl.BlockSpec(memory_space=pltpu.VMEM)
    return pl.pallas_call(
        functools.partial(final_kernel, frame_count),
        out_shape=[pltpu.HBM(omega.shape, jnp.float32)] * 2,
        in_specs=[pl.BlockSpec(memory_space=pltpu.SMEM)] + [vmem] * (2 + len(panels)),
        out_specs=[pl.BlockSpec(memory_space=pltpu.HBM)] * 2,
        scratch_shapes=[wide] * 4
        + [pltpu.VMEM(omega.shape, jnp.float32)] * 2
        + [pltpu.SemaphoreType.DMA((2 * (rows // TILE) ** 2,))],
        compiler_params=pltpu.CompilerParams(vmem_limit_bytes=28 * 1024 * 1024),
        cost_estimate=pl.CostEstimate(flops=4 * rows * rows * frame_count * 3, bytes_accessed=12 * rows * rows, transcendentals=0),
    )(place, pltpu.with_memory_space_constraint(omega, pltpu.VMEM), xc, *panels)


def swap_cols(value, mask):
    return lax.ppermute(value, "cols", [(i, i ^ mask) for i in range(SIDE)])


def swap_rows(value, mask):
    return lax.ppermute(value, "rows", [(i, i ^ mask) for i in range(SIDE)])


ROWS = (
    "8bf5137eda064c92",
    "a9c6104efb7d2583",
    "7ca9f6134ed8b025",
    "db854e20f69c1a73",
    "46b1fa3c85d02e79",
    "7582de094ab13fc6",
    "a07539ed4fb628c1",
    "b16428cfe5a3790d",
    "2f68b5c031e49a7d",
    "e3ad4917205f8bc6",
    "38f04e97c5216dab",
    "28d15fa67e0493cb",
    "c9ad3650fe2b4781",
    "8ef4721bdc90563a",
    "7cdb821409efa356",
    "e9af365072bcd814",
)


LANDING = {(r, c): (int(ROWS[r][c], SIDE), r) for r in range(SIDE) for c in range(SIDE)}
SOURCE = {there: here for here, there in LANDING.items()}


def slots():
    table = np.zeros((SIDE, SIDE, 4, SIDE), np.int32)
    for r in range(SIDE):
        for c in range(SIDE):
            found = {}
            for hop in range(4):
                near = SOURCE[r ^ hop, c][1]
                for y in range(4):
                    found[near & 9 | y << 1] = hop * 4 + y, hop * 4 + (y ^ (near >> 1 & 3))
            for q in range(SIDE):
                y = (q >> 1) & 3
                side = ((q ^ c) & 1) * 8 + ((q ^ c) >> 3) * 4
                table[r, c, 0, q] = found[q][1]
                table[r, c, 1, q] = side + (y ^ ((c >> 1) & 3))
                table[r, c, 2, q] = found[q][0]
                table[r, c, 3, q] = side + y
    return table.reshape(SIDE, SIDE, 4 * SIDE)


def sum_near(sums):
    value = sums[:8] + swap_cols(sums[8:], 1)
    value = value[:4] + swap_cols(value[4:], 8)
    others = [swap_cols(value, 2 * m) for m in (1, 2, 3)]
    return (value + others[0]) + (others[1] + others[2])


def gather_near(piece):
    value = piece[None]
    return jnp.concatenate([value] + [swap_cols(value, 2 * m) for m in (1, 2, 3)], 0)


def turn(four, beside=None):
    pairs = [(r * SIDE + c, LANDING[r, c][0] * SIDE + LANDING[r, c][1]) for r in range(SIDE) for c in range(SIDE)]
    turned = lax.ppermute(four, ("rows", "cols"), pairs)
    if beside is not None:
        turned, beside = lax.optimization_barrier((turned, beside))
    panel = jnp.concatenate([turned] + [swap_rows(turned, m) for m in (1, 2, 3)], 0)
    return panel if beside is None else (panel, beside)


def along(four):
    value = jnp.concatenate([four, swap_cols(four, 8)], 0)
    return jnp.concatenate([value, swap_cols(value, 1)], 0)


def on_device(frames, precision):
    row, col = lax.axis_index("rows"), lax.axis_index("cols")
    table = lax.dynamic_slice(jnp.asarray(slots()), (row, col, 0), (1, 1, 4 * SIDE)).reshape(-1)
    place = jnp.concatenate([jnp.stack([row, col]).astype(jnp.int32), table])
    own = gather_near(frames.T)
    own, begun = lax.optimization_barrier((own, precision))
    xc, current = turn(own, staged(begun))
    xr = along(own)
    (sums,) = sweep(place, current, xc, ())
    for index in range(ITERS):
        four = sum_near(sums)
        yc = turn(four)
        yr = along(four)
        if index < ITERS - 1:
            current, sums = sweep(place, current, xc, (xr, yr, yc))
        else:
            current, gradient = final_sweep(place, current, xc, (xr, yr, yc))
    return (current, gradient)


def solution(mesh):
    placed = (P(None, ("rows", "cols")), P("rows", "cols"))
    return jax.shard_map(
        on_device,
        mesh=mesh,
        in_specs=placed,
        out_specs=(P("rows", "cols"), P("rows", "cols")),
        check_vma=False,
    )
```

```python
import functools

import jax
import jax.numpy as jnp
import numpy as np
from jax import lax
from jax.experimental import pallas as pl
from jax.experimental.pallas import tpu as pltpu
from jax.sharding import PartitionSpec as P

ITERS = 3

step_size = 0.005
penalty = 4.0

SIDE = 16
PIECE = 64
TILE = 512
FETCHES = 8
NT = (((1,), (1,)), ((), ()))


def split(value):
    high = value.astype(jnp.bfloat16)
    low = (value - high.astype(jnp.float32)).astype(jnp.bfloat16)
    return high, low


def dot(a, b, dims=(((1,), (0,)), ((), ()))):
    return lax.dot_general(a, b, dims, preferred_element_type=jnp.float32)


def load_panels(update, emit_sums, frame_count, place, xc, xr, yr, yc, ah, al, bh, bl, xx):
    for slot in range(SIDE):
        q = place[2 + slot]
        span = pl.ds(pl.multiple_of(q * PIECE, PIECE), PIECE)
        high, low = split(xc[slot // 4][slot % 4])
        if emit_sums:
            xx[span, :frame_count] = high
            xx[span, frame_count:] = low
        if update:
            bh[span, :frame_count] = high
            bl[span, :frame_count] = low
            for panel, first, left, right, columns, width in (
                (yc, 34, bh, bl, slice(frame_count, None), 4),
                (yr, 50, ah, al, slice(None, frame_count), 8),
                (xr, 18, ah, al, slice(frame_count, None), 8),
            ):
                q = place[first + slot]
                span = pl.ds(pl.multiple_of(q * PIECE, PIECE), PIECE)
                high, low = split(panel[slot // width][slot % width])
                left[span, columns] = high
                right[span, columns] = low


def gradient_part(frame_count, a_high, a_low, b_high, b_low):
    return (dot(a_high, b_high, NT) + dot(a_high, b_low, NT) + dot(a_low, b_high, NT)) * (0.5 / frame_count)


def step(old, g, eye):
    bound = step_size * penalty
    if eye is not None:
        g = g - jnp.where(eye, 1.0 / jnp.where(eye, old, 1.0), 0.0)
    moved = old - step_size * g
    cut = jnp.clip(moved, -bound, bound)
    if eye is not None:
        cut = jnp.where(eye, 0.0, cut)
    return g, moved - cut


def diagonal(on):
    eye = lax.broadcasted_iota(jnp.int32, (TILE, TILE), 0) == lax.broadcasted_iota(jnp.int32, (TILE, TILE), 1)
    return jnp.logical_and(eye, on)


def sweep_kernel(update, frame_count, *refs):
    if update:
        place, omega, *panels, out, sums, ah, al, bh, bl, xx = refs
        xc, xr, yr, yc = panels[:4], panels[4:6], panels[6:8], panels[8:]
        load_panels(True, True, frame_count, place, xc, xr, yr, yc, ah, al, bh, bl, xx)
    else:
        place, omega, *xc, sums, xx = refs
        load_panels(False, True, frame_count, place, xc, None, None, None, None, None, None, None, xx)
    rows = omega.shape[0]
    col = place[1]
    here = place[0] == col
    for t in range(rows // TILE):
        mine = slice(t * TILE, t * TILE + TILE)
        both = rest = None
        for j in range(rows // TILE):
            span = slice(j * TILE, j * TILE + TILE)
            value = omega[mine, span]
            if update:
                g = gradient_part(frame_count, ah[mine, :], al[mine, :], bh[span, :], bl[span, :])
                _, value = step(value, g, diagonal(here) if j == t else None)
                out[mine, span] = value
            high, low = split(value)
            first = dot(high, xx[span, :])
            second = dot(low, xx[span, :frame_count])
            both = first if both is None else both + first
            rest = second if rest is None else rest + second
        total = both[:, :frame_count] + both[:, frame_count:] + rest
        for s in range(TILE // PIECE):
            q = t * (TILE // PIECE) + s
            slot = ((q ^ col) & 1) * 8 + ((q ^ col) >> 3) * 4 + ((q >> 1) & 3)
            sums[slot] = total[s * PIECE : (s + 1) * PIECE]


def sweep(place, omega, xc, panels):
    update = bool(panels)
    rows = omega.shape[0]
    frame_count = xc[0].shape[-1]
    wide = pltpu.VMEM((rows, 2 * frame_count), jnp.bfloat16)
    vmem = pl.BlockSpec(memory_space=pltpu.VMEM)
    shapes = [jax.ShapeDtypeStruct((SIDE, PIECE, frame_count), jnp.float32)]
    if update:
        shapes = [pltpu.VMEM(omega.shape, jnp.float32)] + shapes
    return pl.pallas_call(
        functools.partial(sweep_kernel, update, frame_count),
        out_shape=shapes,
        in_specs=[pl.BlockSpec(memory_space=pltpu.SMEM)] + [vmem] * (1 + len(xc) + len(panels)),
        out_specs=[vmem] * len(shapes),
        scratch_shapes=[wide] * (5 if update else 1),
        compiler_params=pltpu.CompilerParams(vmem_limit_bytes=28 * 1024 * 1024),
        cost_estimate=pl.CostEstimate(flops=4 * rows * rows * frame_count * 3, bytes_accessed=8 * rows * rows, transcendentals=0),
    )(place, pltpu.with_memory_space_constraint(omega, pltpu.VMEM), *xc, *panels)


def stage_kernel(whole, held, arrived):
    step_rows = whole.shape[0] // FETCHES
    copies = []
    for n in range(FETCHES):
        part = pl.ds(n * step_rows, step_rows)
        copies.append(pltpu.make_async_copy(whole.at[part, :], held.at[part, :], arrived.at[n]))
        copies[-1].start()
    for copy in copies:
        copy.wait()


def staged(omega):
    return pl.pallas_call(
        stage_kernel,
        out_shape=pltpu.VMEM(omega.shape, jnp.float32),
        in_specs=[pl.BlockSpec(memory_space=pltpu.HBM)],
        out_specs=pl.BlockSpec(memory_space=pltpu.VMEM),
        scratch_shapes=[pltpu.SemaphoreType.DMA((FETCHES,))],
        compiler_params=pltpu.CompilerParams(vmem_limit_bytes=4 * 1024 * 1024),
        cost_estimate=pl.CostEstimate(flops=0, bytes_accessed=8 * omega.size, transcendentals=0),
    )(pltpu.with_memory_space_constraint(omega, pltpu.HBM))


def final_kernel(frame_count, place, omega, *refs):
    *panels, out, grad, ah, al, bh, bl, values, grads, sent = refs
    xc, xr, yr, yc = panels[:4], panels[4:6], panels[6:8], panels[8:]
    load_panels(True, False, frame_count, place, xc, xr, yr, yc, ah, al, bh, bl, None)
    rows = omega.shape[0]
    here = place[0] == place[1]
    copies = []
    for t in range(rows // TILE):
        mine = slice(t * TILE, t * TILE + TILE)
        for j in range(rows // TILE):
            span = slice(j * TILE, j * TILE + TILE)
            g = gradient_part(frame_count, ah[mine, :], al[mine, :], bh[span, :], bl[span, :])
            g, value = step(omega[mine, span], g, diagonal(here) if j == t else None)
            grads[mine, span] = g
            values[mine, span] = value
            for held, there in ((grads, grad), (values, out)):
                block = (pl.ds(t * TILE, TILE), pl.ds(j * TILE, TILE))
                copies.append(pltpu.make_async_copy(held.at[block], there.at[block], sent.at[len(copies)]))
                copies[-1].start()
    for copy in copies:
        copy.wait()


def final_sweep(place, omega, xc, panels):
    rows = omega.shape[0]
    frame_count = xc[0].shape[-1]
    wide = pltpu.VMEM((rows, 2 * frame_count), jnp.bfloat16)
    vmem = pl.BlockSpec(memory_space=pltpu.VMEM)
    return pl.pallas_call(
        functools.partial(final_kernel, frame_count),
        out_shape=[pltpu.HBM(omega.shape, jnp.float32)] * 2,
        in_specs=[pl.BlockSpec(memory_space=pltpu.SMEM)] + [vmem] * (1 + len(xc) + len(panels)),
        out_specs=[pl.BlockSpec(memory_space=pltpu.HBM)] * 2,
        scratch_shapes=[wide] * 4
        + [pltpu.VMEM(omega.shape, jnp.float32)] * 2
        + [pltpu.SemaphoreType.DMA((2 * (rows // TILE) ** 2,))],
        compiler_params=pltpu.CompilerParams(vmem_limit_bytes=28 * 1024 * 1024),
        cost_estimate=pl.CostEstimate(flops=4 * rows * rows * frame_count * 3, bytes_accessed=12 * rows * rows, transcendentals=0),
    )(place, pltpu.with_memory_space_constraint(omega, pltpu.VMEM), *xc, *panels)


def swap_cols(value, mask):
    return lax.ppermute(value, "cols", [(i, i ^ mask) for i in range(SIDE)])


def swap_rows(value, mask):
    return lax.ppermute(value, "rows", [(i, i ^ mask) for i in range(SIDE)])


ROWS = (
    "8bf5137eda064c92",
    "a9c6104efb7d2583",
    "7ca9f6134ed8b025",
    "db854e20f69c1a73",
    "46b1fa3c85d02e79",
    "7582de094ab13fc6",
    "a07539ed4fb628c1",
    "b16428cfe5a3790d",
    "2f68b5c031e49a7d",
    "e3ad4917205f8bc6",
    "38f04e97c5216dab",
    "28d15fa67e0493cb",
    "c9ad3650fe2b4781",
    "8ef4721bdc90563a",
    "7cdb821409efa356",
    "e9af365072bcd814",
)


LANDING = {(r, c): (int(ROWS[r][c], SIDE), r) for r in range(SIDE) for c in range(SIDE)}
SOURCE = {there: here for here, there in LANDING.items()}


def slots():
    table = np.zeros((SIDE, SIDE, 4, SIDE), np.int32)
    for r in range(SIDE):
        for c in range(SIDE):
            found = {}
            for hop in range(4):
                near = SOURCE[r ^ hop, c][1]
                for y in range(4):
                    found[near & 9 | y << 1] = hop * 4 + y, hop * 4 + (y ^ (near >> 1 & 3))
            for q in range(SIDE):
                y = (q >> 1) & 3
                side = ((q ^ c) & 1) * 8 + ((q ^ c) >> 3) * 4
                table[r, c, 0, q] = found[q][1]
                table[r, c, 1, q] = side + (y ^ ((c >> 1) & 3))
                table[r, c, 2, q] = found[q][0]
                table[r, c, 3, q] = side + y
    return np.argsort(table, -1).astype(np.int32).reshape(SIDE, SIDE, 4 * SIDE)


def sum_near(sums):
    value = sums[:8] + swap_cols(sums[8:], 1)
    value = value[:4] + swap_cols(value[4:], 8)
    others = [swap_cols(value, 2 * m) for m in (1, 2, 3)]
    return (value + others[0]) + (others[1] + others[2])


def gather_near(piece):
    value = piece[None]
    return jnp.concatenate([value] + [swap_cols(value, 2 * m) for m in (1, 2, 3)], 0)


def turn(four, beside=None):
    pairs = [(r * SIDE + c, LANDING[r, c][0] * SIDE + LANDING[r, c][1]) for r in range(SIDE) for c in range(SIDE)]
    turned = lax.ppermute(four, ("rows", "cols"), pairs)
    if beside is not None:
        turned, beside = lax.optimization_barrier((turned, beside))
    panel = [turned] + [swap_rows(turned, m) for m in (1, 2, 3)]
    return panel if beside is None else (panel, beside)


def along(four):
    value = jnp.concatenate([four, swap_cols(four, 8)], 0)
    return [value, swap_cols(value, 1)]


def on_device(frames, precision):
    row, col = lax.axis_index("rows"), lax.axis_index("cols")
    table = lax.dynamic_slice(jnp.asarray(slots()), (row, col, 0), (1, 1, 4 * SIDE)).reshape(-1)
    place = jnp.concatenate([jnp.stack([row, col]).astype(jnp.int32), table])
    own = gather_near(frames.T)
    own, begun = lax.optimization_barrier((own, precision))
    xc, current = turn(own, staged(begun))
    xr = along(own)
    (sums,) = sweep(place, current, xc, ())
    for index in range(ITERS):
        four = sum_near(sums)
        yc = turn(four)
        yr = along(four)
        if index < ITERS - 1:
            current, sums = sweep(place, current, xc, (*xr, *yr, *yc))
        else:
            current, gradient = final_sweep(place, current, xc, (*xr, *yr, *yc))
    return (current, gradient)


def solution(mesh):
    placed = (P(None, ("rows", "cols")), P("rows", "cols"))
    return jax.shard_map(
        on_device,
        mesh=mesh,
        in_specs=placed,
        out_specs=(P("rows", "cols"), P("rows", "cols")),
        check_vma=False,
    )
```

```python
import functools

import jax
import jax.numpy as jnp
import numpy as np
from jax import lax
from jax.experimental import pallas as pl
from jax.experimental.pallas import tpu as pltpu
from jax.sharding import PartitionSpec as P

ITERS = 3

step_size = 0.005
penalty = 4.0

SIDE = 16
PIECE = 64
TILE = 512
FETCHES = 8
NT = (((1,), (1,)), ((), ()))


def split(value):
    high = value.astype(jnp.bfloat16)
    low = (value - high.astype(jnp.float32)).astype(jnp.bfloat16)
    return high, low


def dot(a, b, dims=(((1,), (0,)), ((), ()))):
    return lax.dot_general(a, b, dims, preferred_element_type=jnp.float32)


def load_panels(update, emit_sums, frame_count, place, xc, xr, yr, yc, ah, al, bh, bl, xx):
    for q in range(SIDE):
        span = pl.ds(q * PIECE, PIECE)
        high, low = split(xc[place[2 + q]])
        if emit_sums:
            xx[span, :frame_count] = high
            xx[span, frame_count:] = low
        if update:
            bh[span, :frame_count] = high
            bl[span, :frame_count] = low
            high, low = split(yc[place[34 + q]])
            bh[span, frame_count:] = high
            bl[span, frame_count:] = low
            high, low = split(yr[place[50 + q]])
            ah[span, :frame_count] = high
            al[span, :frame_count] = low
            high, low = split(xr[place[18 + q]])
            ah[span, frame_count:] = high
            al[span, frame_count:] = low


def gradient_part(frame_count, a_high, a_low, b_high, b_low):
    return (dot(a_high, b_high, NT) + dot(a_high, b_low, NT) + dot(a_low, b_high, NT)) * (0.5 / frame_count)


def step(old, g, eye):
    bound = step_size * penalty
    if eye is not None:
        g = g - jnp.where(eye, 1.0 / jnp.where(eye, old, 1.0), 0.0)
    moved = old - step_size * g
    cut = jnp.clip(moved, -bound, bound)
    if eye is not None:
        cut = jnp.where(eye, 0.0, cut)
    return g, moved - cut


def diagonal(on):
    eye = lax.broadcasted_iota(jnp.int32, (TILE, TILE), 0) == lax.broadcasted_iota(jnp.int32, (TILE, TILE), 1)
    return jnp.logical_and(eye, on)


def sweep_kernel(update, frame_count, *refs):
    if update:
        place, omega, xc, xr, yr, yc, out, sums, ah, al, bh, bl, xx = refs
        load_panels(True, True, frame_count, place, xc, xr, yr, yc, ah, al, bh, bl, xx)
    else:
        place, omega, xc, sums, xx = refs
        load_panels(False, True, frame_count, place, xc, None, None, None, None, None, None, None, xx)
    rows = omega.shape[0]
    col = place[1]
    here = place[0] == col
    for t in range(rows // TILE):
        mine = slice(t * TILE, t * TILE + TILE)
        both = rest = None
        for j in range(rows // TILE):
            span = slice(j * TILE, j * TILE + TILE)
            value = omega[mine, span]
            if update:
                g = gradient_part(frame_count, ah[mine, :], al[mine, :], bh[span, :], bl[span, :])
                _, value = step(value, g, diagonal(here) if j == t else None)
                out[mine, span] = value
            high, low = split(value)
            first = dot(high, xx[span, :])
            second = dot(low, xx[span, :frame_count])
            both = first if both is None else both + first
            rest = second if rest is None else rest + second
        total = both[:, :frame_count] + both[:, frame_count:] + rest
        for s in range(TILE // PIECE):
            q = t * (TILE // PIECE) + s
            slot = ((q ^ col) & 1) * 8 + ((q ^ col) >> 3) * 4 + ((q >> 1) & 3)
            sums[slot] = total[s * PIECE : (s + 1) * PIECE]


def sweep(place, omega, xc, panels):
    update = bool(panels)
    rows = omega.shape[0]
    frame_count = xc.shape[-1]
    wide = pltpu.VMEM((rows, 2 * frame_count), jnp.bfloat16)
    vmem = pl.BlockSpec(memory_space=pltpu.VMEM)
    shapes = [jax.ShapeDtypeStruct((SIDE, PIECE, frame_count), jnp.float32)]
    if update:
        shapes = [pltpu.VMEM(omega.shape, jnp.float32)] + shapes
    return pl.pallas_call(
        functools.partial(sweep_kernel, update, frame_count),
        out_shape=shapes,
        in_specs=[pl.BlockSpec(memory_space=pltpu.SMEM)] + [vmem] * (2 + len(panels)),
        out_specs=[vmem] * len(shapes),
        scratch_shapes=[wide] * (5 if update else 1),
        compiler_params=pltpu.CompilerParams(vmem_limit_bytes=28 * 1024 * 1024),
        cost_estimate=pl.CostEstimate(flops=4 * rows * rows * frame_count * 3, bytes_accessed=8 * rows * rows, transcendentals=0),
    )(place, pltpu.with_memory_space_constraint(omega, pltpu.VMEM), xc, *panels)


def stage_kernel(whole, held, arrived):
    step_rows = whole.shape[0] // FETCHES
    copies = []
    for n in range(FETCHES):
        part = pl.ds(n * step_rows, step_rows)
        copies.append(pltpu.make_async_copy(whole.at[part, :], held.at[part, :], arrived.at[n]))
        copies[-1].start()
    for copy in copies:
        copy.wait()


def staged(omega):
    return pl.pallas_call(
        stage_kernel,
        out_shape=pltpu.VMEM(omega.shape, jnp.float32),
        in_specs=[pl.BlockSpec(memory_space=pltpu.HBM)],
        out_specs=pl.BlockSpec(memory_space=pltpu.VMEM),
        scratch_shapes=[pltpu.SemaphoreType.DMA((FETCHES,))],
        compiler_params=pltpu.CompilerParams(vmem_limit_bytes=4 * 1024 * 1024),
        cost_estimate=pl.CostEstimate(flops=0, bytes_accessed=8 * omega.size, transcendentals=0),
    )(pltpu.with_memory_space_constraint(omega, pltpu.HBM))


def final_kernel(frame_count, place, omega, xc, xr, yr, yc, out, grad, ah, al, bh, bl, values, grads, sent):
    load_panels(True, False, frame_count, place, xc, xr, yr, yc, ah, al, bh, bl, None)
    rows = omega.shape[0]
    here = place[0] == place[1]
    copies = []
    for t in range(rows // TILE):
        mine = slice(t * TILE, t * TILE + TILE)
        for j in range(rows // TILE):
            span = slice(j * TILE, j * TILE + TILE)
            g = gradient_part(frame_count, ah[mine, :], al[mine, :], bh[span, :], bl[span, :])
            g, value = step(omega[mine, span], g, diagonal(here) if j == t else None)
            grads[mine, span] = g
            values[mine, span] = value
            for held, there in ((grads, grad), (values, out)):
                block = (pl.ds(t * TILE, TILE), pl.ds(j * TILE, TILE))
                copies.append(pltpu.make_async_copy(held.at[block], there.at[block], sent.at[len(copies)]))
                copies[-1].start()
    for copy in copies:
        copy.wait()


def final_sweep(place, omega, xc, panels):
    rows = omega.shape[0]
    frame_count = xc.shape[-1]
    wide = pltpu.VMEM((rows, 2 * frame_count), jnp.bfloat16)
    vmem = pl.BlockSpec(memory_space=pltpu.VMEM)
    return pl.pallas_call(
        functools.partial(final_kernel, frame_count),
        out_shape=[pltpu.HBM(omega.shape, jnp.float32)] * 2,
        in_specs=[pl.BlockSpec(memory_space=pltpu.SMEM)] + [vmem] * (2 + len(panels)),
        out_specs=[pl.BlockSpec(memory_space=pltpu.HBM)] * 2,
        scratch_shapes=[wide] * 4
        + [pltpu.VMEM(omega.shape, jnp.float32)] * 2
        + [pltpu.SemaphoreType.DMA((2 * (rows // TILE) ** 2,))],
        compiler_params=pltpu.CompilerParams(vmem_limit_bytes=28 * 1024 * 1024),
        cost_estimate=pl.CostEstimate(flops=4 * rows * rows * frame_count * 3, bytes_accessed=12 * rows * rows, transcendentals=0),
    )(place, pltpu.with_memory_space_constraint(omega, pltpu.VMEM), xc, *panels)


def swap_cols(value, mask):
    return lax.ppermute(value, "cols", [(i, i ^ mask) for i in range(SIDE)])


def swap_rows(value, mask):
    return lax.ppermute(value, "rows", [(i, i ^ mask) for i in range(SIDE)])


ROWS = (
    "8bf5137eda064c92",
    "a9c6104efb7d2583",
    "7ca9f6134ed8b025",
    "db854e20f69c1a73",
    "46b1fa3c85d02e79",
    "7582de094ab13fc6",
    "a07539ed4fb628c1",
    "b16428cfe5a3790d",
    "2f68b5c031e49a7d",
    "e3ad4917205f8bc6",
    "38f04e97c5216dab",
    "28d15fa67e0493cb",
    "c9ad3650fe2b4781",
    "8ef4721bdc90563a",
    "7cdb821409efa356",
    "e9af365072bcd814",
)


LANDING = {(r, c): (int(ROWS[r][c], SIDE), r) for r in range(SIDE) for c in range(SIDE)}
SOURCE = {there: here for here, there in LANDING.items()}


def slots():
    table = np.zeros((SIDE, SIDE, 4, SIDE), np.int32)
    for r in range(SIDE):
        for c in range(SIDE):
            found = {}
            for hop in range(4):
                near = SOURCE[r ^ hop, c][1]
                for y in range(4):
                    found[near & 9 | y << 1] = hop * 4 + y, hop * 4 + (y ^ (near >> 1 & 3))
            for q in range(SIDE):
                y = (q >> 1) & 3
                side = ((q ^ c) & 1) * 8 + ((q ^ c) >> 3) * 4
                table[r, c, 0, q] = found[q][1]
                table[r, c, 1, q] = side + (y ^ ((c >> 1) & 3))
                table[r, c, 2, q] = found[q][0]
                table[r, c, 3, q] = side + y
    return table.reshape(SIDE, SIDE, 4 * SIDE)


def sum_near(sums):
    value = sums[:8] + swap_cols(sums[8:], 1)
    value = value[:4] + swap_cols(value[4:], 8)
    others = [swap_cols(value, 2 * m) for m in (1, 2, 3)]
    return (value + others[0]) + (others[1] + others[2])


def gather_near(piece):
    value = piece[None]
    return jnp.concatenate([value] + [swap_cols(value, 2 * m) for m in (1, 2, 3)], 0)


def turn(four, beside=None):
    pairs = [(r * SIDE + c, LANDING[r, c][0] * SIDE + LANDING[r, c][1]) for r in range(SIDE) for c in range(SIDE)]
    turned = lax.ppermute(four, ("rows", "cols"), pairs)
    if beside is not None:
        turned, beside = lax.optimization_barrier((turned, beside))
    panel = jnp.concatenate([turned] + [swap_rows(turned, m) for m in (1, 2, 3)], 0)
    return panel if beside is None else (panel, beside)


def along(four):
    return jnp.concatenate([four] + [swap_cols(four, m) for m in (8, 1, 9)], 0)


def on_device(frames, precision):
    row, col = lax.axis_index("rows"), lax.axis_index("cols")
    table = lax.dynamic_slice(jnp.asarray(slots()), (row, col, 0), (1, 1, 4 * SIDE)).reshape(-1)
    place = jnp.concatenate([jnp.stack([row, col]).astype(jnp.int32), table])
    own = gather_near(frames.T)
    own, begun = lax.optimization_barrier((own, precision))
    xc, current = turn(own, staged(begun))
    xr = along(own)
    (sums,) = sweep(place, current, xc, ())
    for index in range(ITERS):
        four = sum_near(sums)
        yc = turn(four)
        yr = along(four)
        if index < ITERS - 1:
            current, sums = sweep(place, current, xc, (xr, yr, yc))
        else:
            current, gradient = final_sweep(place, current, xc, (xr, yr, yc))
    return (current, gradient)


def solution(mesh):
    placed = (P(None, ("rows", "cols")), P("rows", "cols"))
    return jax.shard_map(
        on_device,
        mesh=mesh,
        in_specs=placed,
        out_specs=(P("rows", "cols"), P("rows", "cols")),
        check_vma=False,
    )
```
